32 devices in a mesh: replica: 1, expert: 16 (over z, y, x), tensor: 2 (over core).
Axes of the slice: x: 2, y: 2, z: 4, core: 2. Of those that a mesh axis runs over, the one named last changes fastest.
Arguments:
- token_values: bfloat16 [1024, 4096], P(('replica', 'expert'), 'tensor'), may hold values from -6 to 6
- token_scales: bfloat16 [1024, 32], P(('replica', 'expert'), 'tensor'), may hold values from 0.19921875 to 2.5
- expert_ids: int32 [1024, 8], P(('replica', 'expert')), may hold values from 0 to 15, all different within a row; in each aligned block of 64 rows (0 to 63, 64 to 127, ...) at most 40 rows name the same one
- route_weights: int32 [1024, 8], P(('replica', 'expert')), may hold values from 1 to 4095
- gate_weight: bfloat16 [16, 4096, 768], P('expert', None, 'tensor'), may hold values from -0.09375 to 0.09375
- up_weight: bfloat16 [16, 4096, 768], P('expert', None, 'tensor'), may hold values from -0.09375 to 0.09375
- down_weight: bfloat16 [16, 768, 4096], P('expert', 'tensor'), may hold values from -0.21875 to 0.21875
Outputs:
- mixed: bfloat16 [1024, 4096], P(('replica', 'expert'), 'tensor')
The draws below stay inside these ranges and needn't reach their ends.
Inputs may be any that keep to these rules, and one draw needn't show every extreme that they name: `expert_ids`: each row names 8 different experts. In each aligned block of 64 rows (the tokens of one index of expert) no expert is named by more than 40 rows, a bound that some block reaches.
All inputs are finite; a program needn't handle non-finite values.
Results may differ from the reference program's by a relative error of at most 0.0076.
Values may be sent and summed in bfloat16 or wider, within the bound.
No kernel may reach another device: no remote copies, remote signals or barrier semaphores. Data moves between devices by JAX's collectives and lax.ppermute only.
A program may use at most 128 MiB of HBM per device.

```python
import math
import jax
import jax.numpy as jnp
import numpy as np
from jax import lax

D = 4096
FFW = 768
TOP = 8
SCALE_BLOCK = 128
WALSH = 128
TOK_DEV = 64
EXPERTS = 16
TOKENS = 1024
CAP = 40
N_EXPERT = 16


def touch_ends(entries, key, least, largest):
    extent = entries.shape
    index_at = [jax.random.randint(jax.random.fold_in(key, axis), (), 0, extent[axis]) for axis in range(len(extent))]
    entries = entries.at[tuple(index_at)].set(least)
    longest = extent.index(max(extent))
    index_at[longest] = (index_at[longest] + 1) % extent[longest]
    return entries.at[tuple(index_at)].set(largest)


def level_of(key, extent, split, low, largest):
    def one(position, parts):
        steps = jax.random.uniform(jax.random.fold_in(jax.random.fold_in(key, 6), position), (parts,), jnp.float32, low / len(split), largest / len(split))
        return jnp.repeat(jnp.exp(steps), extent[position] // parts).reshape((-1,) + (1,) * (len(extent) - position - 1))

    level = one(*split[0])
    for cut in split[1:]:
        level = level * one(*cut)
    return level


def deal_out(rng, own, number, rows, count, top, bound, skew):
    sequence = jax.random.permutation(rng, count)
    crowded, ordinary = portions_of(count, rows * top, bound, skew, True), portions_of(count, rows * top, bound, skew, False)
    places = jnp.arange(count)

    def named(sizes, turn):
        used = int((sizes > 0).sum())
        fixed = max(1, used // 4)
        passed = fixed + (places - fixed + turn * (used - fixed)) % max(1, count - fixed)
        return jnp.zeros((count,), jnp.int32).at[sequence[jnp.where(places < fixed, places, passed)]].set(jnp.asarray(sizes, jnp.int32))

    sizes = jnp.where(number % 4 == 0, named(crowded, number // 4), named(ordinary, number - number // 4 - 1))
    mixed = jax.random.permutation(jax.random.fold_in(own, 3), count)
    donor, taker = mixed[0:count // 2 * 2:2], mixed[1:count // 2 * 2:2]
    room = jnp.minimum(sizes[donor] - 1, bound - sizes[taker]) // 2
    room = jnp.where((donor == sequence[0]) | (taker == sequence[0]) | (sizes[taker] == 0), 0, jnp.maximum(room, 0))
    passed = jax.random.randint(jax.random.fold_in(own, 4), (count // 2,), 0, 1 << 20) % (room + 1)
    sizes = sizes.at[donor].add(-passed).at[taker].add(passed)
    items = jnp.searchsorted(jnp.cumsum(sizes), jnp.arange(rows * top), side="right").astype(jnp.int32)
    grid = items.reshape(top, rows).T
    grid = grid[jax.random.permutation(jax.random.fold_in(own, 1), rows)]
    turn = jax.random.randint(jax.random.fold_in(own, 2), (rows, 1), 0, top)
    return jnp.take_along_axis(grid, (jnp.arange(top)[None, :] + turn) % top, axis=1)


def portions_of(count, total, bound, lean, full):
    loads = [(1 << 20) // math.isqrt(grade ** lean) + 1 for grade in range(1, count + 1)]
    largest = bound if full else min(bound, max(-(-total // count), total * loads[0] // sum(loads)))
    least = 1 if total - largest >= count - 1 else 0
    given, spare = [largest] + [least] * (count - 1), total - largest - least * (count - 1)
    while spare > 0:
        free = [i for i in range(1, count) if given[i] < largest] or [i for i in range(1, count) if given[i] < bound]
        pool, left = sum([loads[i] for i in free]), spare
        for i in free:
            addition = min(bound - given[i], max(1, left * loads[i] // pool), spare)
            given[i] = given[i] + addition
            spare = spare - addition
    return np.array(given)


def noise(key, dims, deviation, limit, pieces=(), kind=jnp.bfloat16):
    entries = jax.random.normal(key, dims, jnp.float32) * deviation
    if len(pieces) > 0:
        entries = level_of(key, dims, pieces, -0.22, 0.18) * entries
    return jnp.clip(entries, min=-limit, max=limit).astype(kind)


def setup_inputs(seed: int = 0, part: int = 0) -> dict:
    splits = jax.random.split(jax.random.key(seed), 8)
    part_keys = jax.random.split(jax.random.fold_in(splits[7], part), 8)
    token_values = noise(part_keys[0], (TOKENS, D), 1.0, 6.0, ((0, 16), (1, 2)))
    token_scales = jnp.clip(jnp.exp(math.log(2.5) - 2.5296425 * jax.random.uniform(part_keys[1], (TOKENS, D // SCALE_BLOCK), jnp.float32) ** level_of(part_keys[1], (TOKENS, D // SCALE_BLOCK), ((0, 16), (1, 2)), -0.2, 0.2)), 0.19921875, 2.5).astype(jnp.bfloat16)
    expert_ids_keys = jax.random.split(jax.random.fold_in(part_keys[2], 1), TOKENS // TOK_DEV)
    expert_ids_turns = jax.random.permutation(jax.random.fold_in(part_keys[2], 3), TOKENS // TOK_DEV)
    expert_ids = jax.vmap(lambda own, number: deal_out(jax.random.fold_in(part_keys[2], 2), own, number, TOK_DEV, EXPERTS, TOP, CAP, 2))(expert_ids_keys, expert_ids_turns).reshape((TOKENS, TOP))
    route_weights = touch_ends(jax.random.randint(part_keys[3], (TOKENS, TOP), 1, 4096), jax.random.fold_in(part_keys[3], 1), 1, 4095).astype(jnp.int32)
    gate_weight = noise(splits[4], (EXPERTS, D, FFW), D ** -0.5, 0.09375, ((0, 16), (2, 2)))
    up_weight = noise(splits[5], (EXPERTS, D, FFW), D ** -0.5, 0.09375, ((0, 16), (2, 2)))
    down_weight = noise(splits[6], (EXPERTS, FFW, D), FFW ** -0.5, 0.21875, ((0, 16), (1, 2)))
    return {"token_values": token_values, "token_scales": token_scales, "expert_ids": expert_ids, "route_weights": route_weights, "gate_weight": gate_weight, "up_weight": up_weight, "down_weight": down_weight}


def walsh_signs(length):
    indices = jnp.arange(length, dtype=jnp.int32)
    parity = jnp.zeros((length, length), jnp.int32)
    for bit_index in range(length.bit_length() - 1):
        parity = parity + jnp.bitwise_and(jnp.bitwise_and(jnp.right_shift(indices[:, None], bit_index), jnp.right_shift(indices[None, :], bit_index)), 1)
    return (1 - 2 * (parity % 2)).astype(jnp.float32)

def rotate(hidden):
    row_count = hidden.shape[0]
    groups = FFW // (2 * WALSH)
    widened = hidden.astype(jnp.float32).reshape(row_count, 2, groups, WALSH)
    combined = jnp.stack([widened[:, 0] + widened[:, 1], widened[:, 0] - widened[:, 1]], axis=1)
    norm_factor = 1.0 / math.sqrt(2 * WALSH)
    turned = jnp.einsum('rtgj,kj->rtgk', combined, walsh_signs(WALSH), precision=lax.Precision.HIGHEST) * norm_factor
    return turned.reshape(row_count, FFW).astype(jnp.bfloat16)

def reference(token_values, token_scales, expert_ids, route_weights, gate_weight, up_weight, down_weight):
    blocks = N_EXPERT
    choices_dev = TOK_DEV * TOP
    flat_ids = expert_ids.reshape(blocks, choices_dev)
    onehot = (flat_ids[:, :, None] == jnp.arange(EXPERTS, dtype=jnp.int32)[None, None, :]).astype(jnp.int32)
    slot_index = lax.optimization_barrier(jnp.sum(jnp.cumsum(onehot, axis=1) * onehot, axis=2)) - 1
    owner_token = (jnp.arange(choices_dev, dtype=jnp.int32) // TOP)[None, :] + (jnp.arange(blocks, dtype=jnp.int32) * TOK_DEV)[:, None]
    source = jnp.broadcast_to(jnp.arange(blocks, dtype=jnp.int32)[:, None], (blocks, choices_dev))
    route = route_weights.astype(jnp.float32)
    route = route / lax.optimization_barrier(jnp.sum(route, axis=1, keepdims=True))
    table = jnp.full((EXPERTS, blocks, CAP), TOKENS, jnp.int32).at[flat_ids, source, slot_index].set(owner_token)
    route_table = jnp.zeros((EXPERTS, blocks, CAP), jnp.float32).at[flat_ids, source, slot_index].set(route.reshape(blocks, choices_dev))
    padded_values = jnp.concatenate([token_values, jnp.zeros((1, D), jnp.bfloat16)], axis=0)
    padded_scales = jnp.concatenate([token_scales, jnp.zeros((1, D // SCALE_BLOCK), jnp.bfloat16)], axis=0)

    def expert_step(running, expert_index):
        picked_rows = table[expert_index].reshape(-1)
        values_rows = padded_values[picked_rows].astype(jnp.float32).reshape(-1, D // SCALE_BLOCK, SCALE_BLOCK)
        scale_rows = padded_scales[picked_rows].astype(jnp.float32)[:, :, None]
        dequant = (values_rows * scale_rows).reshape(-1, D).astype(jnp.bfloat16)
        gate_out = jnp.dot(dequant, gate_weight[expert_index], preferred_element_type=jnp.float32)
        up_out = jnp.dot(dequant, up_weight[expert_index], preferred_element_type=jnp.float32)
        hidden = (jax.nn.silu(gate_out) * up_out).astype(jnp.bfloat16)
        rotated = rotate(hidden)
        expert_out = jnp.dot(rotated, down_weight[expert_index], preferred_element_type=jnp.float32).astype(jnp.bfloat16)
        running = running.at[picked_rows].add(route_table[expert_index].reshape(-1)[:, None] * expert_out.astype(jnp.float32))
        return (running, None)
    running, unused = lax.scan(expert_step, jnp.zeros((TOKENS + 1, D), jnp.float32), jnp.arange(EXPERTS, dtype=jnp.int32))
    return running[:TOKENS].astype(jnp.bfloat16)
```

```python
import functools
import math

import jax
import jax.numpy as jnp
from jax import lax
from jax.experimental import pallas as pl
from jax.experimental.pallas import tpu as pltpu
from jax.sharding import PartitionSpec as P

WALSH = 128
LANES = 128


def walsh_signs(length):
    indices = jnp.arange(length, dtype=jnp.int32)
    parity = jnp.zeros((length, length), jnp.int32)
    for bit_index in range(length.bit_length() - 1):
        parity = parity + jnp.bitwise_and(
            jnp.bitwise_and(
                jnp.right_shift(indices[:, None], bit_index),
                jnp.right_shift(indices[None, :], bit_index),
            ),
            1,
        )
    return (1 - 2 * (parity % 2)).astype(jnp.float32)


def swap(array, masks, core=0):
    experts = lax.axis_size("expert")
    pairs = [
        (e * 2 + t, (e ^ masks[t]) * 2 + (t ^ core)) for e in range(experts) for t in range(2)
    ]
    return lax.ppermute(array, ("expert", "tensor"), pairs)


def cost(flops, *arrays):
    size = sum(math.prod(a.shape) * a.dtype.itemsize for a in arrays)
    return pl.CostEstimate(flops=flops, bytes_accessed=size, transcendentals=0)


def scaled_tokens(values, scales, ids, route_weights, experts):
    rows, features = values.shape
    top = ids.shape[1]
    width = features // scales.shape[1]

    def kernel(values_ref, scales_ref, ids_ref, weights_ref, out_ref):
        factor = scales_ref[...].astype(jnp.float32)
        for block in range(scales.shape[1]):
            cols = slice(block * width, (block + 1) * width)
            out_ref[:, cols] = (
                values_ref[:, cols].astype(jnp.float32) * factor[:, block : block + 1]
            ).astype(jnp.bfloat16)
        weights = weights_ref[...].astype(jnp.float32)
        route = weights / jnp.sum(weights, axis=1, keepdims=True)
        lane = lax.broadcasted_iota(jnp.int32, (rows, LANES), 1)
        expert = lax.rem(lane, experts)
        table = jnp.zeros((rows, LANES), jnp.float32)
        for k in range(top):
            table = table + jnp.where(ids_ref[:, k : k + 1] == expert, route[:, k : k + 1], 0.0)
        high = table.astype(jnp.bfloat16).astype(jnp.float32)
        tail = jnp.where(lane < experts, high, jnp.where(lane < 2 * experts, table - high, 0.0))
        out_ref[:, features:] = tail.astype(jnp.bfloat16)

    return pl.pallas_call(
        kernel,
        out_shape=jax.ShapeDtypeStruct((rows, features + LANES), jnp.bfloat16),
        name="scaled_tokens",
    )(values, scales, ids, route_weights)


def hidden_units(core, near, near_pair, far, far_pair, gate, up):
    rows_near, wide = near.shape
    rows_far = far.shape[0]
    rows = rows_near + rows_far
    block = rows_near // 2
    features, units = gate.shape
    half = features // 2
    step = LANES

    def kernel(core_ref, near_ref, near_pair_ref, far_ref, far_pair_ref, gate_ref, up_ref, out_ref):
        own = pl.multiple_of(core_ref[0] * half, half)
        other = pl.multiple_of((1 - core_ref[0]) * half, half)
        x_own = jnp.concatenate([near_ref[:, :half], far_ref[:, :half]], axis=0)
        x_other = jnp.concatenate(
            [
                near_pair_ref[:block, :half],
                far_pair_ref[:block, :half],
                near_pair_ref[block:, :half],
                far_pair_ref[block:, :half],
            ],
            axis=0,
        )
        w_own = jnp.concatenate([gate_ref[pl.ds(own, half), :], up_ref[pl.ds(own, half), :]], axis=1)
        w_other = jnp.concatenate(
            [gate_ref[pl.ds(other, half), :], up_ref[pl.ds(other, half), :]], axis=1
        )
        both = jnp.dot(x_own, w_own, preferred_element_type=jnp.float32) + jnp.dot(
            x_other, w_other, preferred_element_type=jnp.float32
        )
        gate_out, up_out = both[:, :step], both[:, step:]
        out_ref[...] = (gate_out / (1.0 + jnp.exp(-gate_out)) * up_out).astype(jnp.bfloat16)

    whole = lambda n: pl.BlockSpec((n, wide), lambda j, core: (0, 0))
    return pl.pallas_call(
        kernel,
        grid_spec=pltpu.PrefetchScalarGridSpec(
            num_scalar_prefetch=1,
            grid=(units // step,),
            in_specs=[
                whole(rows_near),
                whole(rows_near),
                whole(rows_far),
                whole(rows_far),
                pl.BlockSpec((features, step), lambda j, core: (0, j)),
                pl.BlockSpec((features, step), lambda j, core: (0, j)),
            ],
            out_specs=pl.BlockSpec((rows, step), lambda j, core: (0, j)),
        ),
        out_shape=jax.ShapeDtypeStruct((rows, units), jnp.bfloat16),
        compiler_params=pltpu.CompilerParams(vmem_limit_bytes=32 << 20),
        cost_estimate=cost(4 * rows * features * units, near, near, far, far, gate, up),
        name="hidden_units",
    )(core, near, near_pair, far, far_pair, gate, up)


def routed_outputs(core, mine, theirs, mix, down, down_pair, near, far, lanes):
    rows, units = mine.shape
    features = down_pair.shape[1]
    groups = units // WALSH
    split = near.shape[0]
    block = split // 2
    step = min(512, features)
    steps = features // step

    def kernel(core_ref, mine_ref, theirs_ref, mix_ref, down_ref, pair_ref, near_ref, far_ref,
               lanes_ref, near_out, far_out, turned, route):
        @pl.when(pl.program_id(0) == 0)
        def _():
            for g in range(groups):
                cols = slice(g * WALSH, (g + 1) * WALSH)
                other = theirs_ref[:, cols]
                other = jnp.concatenate(
                    [other[:block], other[split : split + block], other[block:split],
                     other[split + block :]],
                    axis=0,
                )
                both = jnp.dot(
                    jnp.concatenate([mine_ref[:, cols], other], axis=1),
                    mix_ref[...],
                    preferred_element_type=jnp.float32,
                ).astype(jnp.bfloat16)
                turned[:, cols] = both[:, :WALSH]
                turned[:, units + g * WALSH : units + (g + 1) * WALSH] = both[:, WALSH:]
            tails = jnp.concatenate([near_ref[...], far_ref[...]], axis=0).astype(jnp.float32)
            weight = jnp.sum(tails * lanes_ref[...], axis=1, keepdims=True)
            route[...] = jnp.broadcast_to(weight, route.shape)

        out = jnp.dot(
            turned[...],
            jnp.concatenate([down_ref[...], pair_ref[...]], axis=0),
            preferred_element_type=jnp.float32,
        )
        scaled = (out * route[:, :1]).astype(jnp.bfloat16)
        near_out[...] = scaled[:split]
        far_out[...] = scaled[split:]

    tail = features // LANES
    return pl.pallas_call(
        kernel,
        grid_spec=pltpu.PrefetchScalarGridSpec(
            num_scalar_prefetch=1,
            grid=(steps,),
            in_specs=[
                pl.BlockSpec((rows, units), lambda j, core: (0, 0)),
                pl.BlockSpec((rows, units), lambda j, core: (0, 0)),
                pl.BlockSpec(mix.shape, lambda j, core: (0, 0)),
                pl.BlockSpec((units, step), lambda j, core: (0, core[0] * steps + j)),
                pl.BlockSpec((units, step), lambda j, core: (0, j)),
                pl.BlockSpec((split, LANES), lambda j, core: (0, tail)),
                pl.BlockSpec((rows - split, LANES), lambda j, core: (0, tail)),
                pl.BlockSpec((1, LANES), lambda j, core: (0, 0)),
            ],
            out_specs=[
                pl.BlockSpec((split, step), lambda j, core: (0, j)),
                pl.BlockSpec((rows - split, step), lambda j, core: (0, j)),
            ],
            scratch_shapes=[
                pltpu.VMEM((rows, 2 * units), jnp.bfloat16),
                pltpu.VMEM((rows, LANES), jnp.float32),
            ],
        ),
        out_shape=[
            jax.ShapeDtypeStruct((split, features), jnp.bfloat16),
            jax.ShapeDtypeStruct((rows - split, features), jnp.bfloat16),
        ],
        compiler_params=pltpu.CompilerParams(vmem_limit_bytes=32 << 20),
        cost_estimate=cost(4 * rows * units * features, mine, theirs, down_pair, down_pair, near, far),
        name="routed_outputs",
    )(core, mine, theirs, mix, down, down_pair, near, far, lanes)


def every_expert(
    token_values, token_scales, expert_ids, route_weights, gate_weight, up_weight, down_weight
):
    experts = lax.axis_size("expert")
    core_index = lax.axis_index("tensor")
    core = core_index.astype(jnp.int32).reshape(1)
    expert = lax.axis_index("expert")
    rows, features = token_values.shape
    gate, up, down = gate_weight[0], up_weight[0], down_weight[0]
    first, second = (1, 2), (2, 1)

    block = scaled_tokens(token_values, token_scales, expert_ids, route_weights, experts)
    blocks = [block] + [swap(block, (m, m)) for m in range(4, experts, 4)]

    other_columns = lax.dynamic_slice(
        down, (0, (1 - core_index) * features), (down.shape[0], features)
    )
    down_pair = swap(other_columns, (0, 0), 1)

    signs = walsh_signs(WALSH) / math.sqrt(2 * WALSH)
    sign = jnp.where(core_index == 0, 1.0, -1.0)
    mix = jnp.concatenate(
        [
            jnp.concatenate([signs * sign, signs], axis=1),
            jnp.concatenate([signs, -signs * sign], axis=1),
        ],
        axis=0,
    ).astype(jnp.bfloat16)
    lane = jnp.arange(LANES, dtype=jnp.int32)[None, :]
    lanes = ((lane % experts == expert) & (lane < 2 * experts)).astype(jnp.float32)

    total = None
    for index, block in enumerate(blocks):
        near = jnp.concatenate([block, swap(block, first)], axis=0)
        far = swap(near, second)
        near_pair = swap(near, (0, 0), 1)
        far_pair = swap(far, (0, 0), 1)
        mine = hidden_units(core, near, near_pair, far, far_pair, gate, up)
        theirs = swap(mine, (0, 0), 1)
        near_out, far_out = routed_outputs(
            core, mine, theirs, mix, down, down_pair, near, far, lanes
        )
        summed = near_out.astype(jnp.float32) + swap(far_out, second).astype(jnp.float32)
        back = swap(summed[rows:].astype(jnp.bfloat16), first).astype(jnp.float32)
        part = summed[:rows] + back
        if index > 0:
            part = swap(part.astype(jnp.bfloat16), (4 * index, 4 * index)).astype(jnp.float32)
        total = part if total is None else total + part
    return total.astype(jnp.bfloat16)


def chosen_experts(
    token_values, token_scales, expert_ids, route_weights, gate_weight, up_weight, down_weight
):
    tok_rows, top_count = expert_ids.shape
    experts = lax.axis_size("expert")
    capacity = min(tok_rows, 5 * tok_rows * top_count // (4 * experts))
    flat_ids = expert_ids.reshape(-1)
    onehot = (flat_ids[:, None] == jnp.arange(experts, dtype=jnp.int32)[None, :]).astype(jnp.int32)
    slot_index = jnp.sum(jnp.cumsum(onehot, axis=0) * onehot, axis=1) - 1
    target = flat_ids * capacity + slot_index
    owner_token = jnp.arange(tok_rows * top_count, dtype=jnp.int32) // top_count
    source = jnp.full((experts * capacity,), tok_rows, jnp.int32).at[target].set(owner_token)
    padded_values = jnp.concatenate(
        [token_values, jnp.zeros((1, token_values.shape[1]), token_values.dtype)], axis=0
    )
    padded_scales = jnp.concatenate(
        [token_scales, jnp.zeros((1, token_scales.shape[1]), token_scales.dtype)], axis=0
    )
    send_values = padded_values[source].reshape(experts, capacity, -1)
    send_scales = padded_scales[source].reshape(experts, capacity, -1)
    arrived_values, arrived_scales = (
        lax.all_to_all(send_values, "expert", split_axis=0, concat_axis=0, tiled=True),
        lax.all_to_all(send_scales, "expert", split_axis=0, concat_axis=0, tiled=True),
    )
    joined_values, joined_scales = (
        lax.all_gather(arrived_values, "tensor", axis=2, tiled=True),
        lax.all_gather(arrived_scales, "tensor", axis=2, tiled=True),
    )
    row_count = experts * capacity
    feature_count = joined_values.shape[2]
    scale_count = joined_scales.shape[2]
    dequant = (
        (
            joined_values.astype(jnp.float32).reshape(
                row_count, scale_count, feature_count // scale_count
            )
            * joined_scales.astype(jnp.float32).reshape(row_count, scale_count, 1)
        )
        .reshape(row_count, feature_count)
        .astype(jnp.bfloat16)
    )
    gate_out = jnp.dot(dequant, gate_weight[0], preferred_element_type=jnp.float32)
    up_out = jnp.dot(dequant, up_weight[0], preferred_element_type=jnp.float32)
    hidden = (jax.nn.silu(gate_out) * up_out).astype(jnp.bfloat16)
    partner = swap(hidden, (0, 0), 1)
    own_part = hidden.astype(jnp.float32)
    theirs = partner.astype(jnp.float32)
    combined = jnp.where(lax.axis_index("tensor") == 0, own_part + theirs, theirs - own_part)
    groups = hidden.shape[1] // WALSH
    norm_factor = 1.0 / math.sqrt(2 * WALSH)
    turned = (
        jnp.einsum(
            "rgj,kj->rgk",
            combined.reshape(row_count, groups, WALSH),
            walsh_signs(WALSH),
            precision=lax.Precision.HIGHEST,
        )
        * norm_factor
    )
    rotated = turned.reshape(row_count, -1).astype(jnp.bfloat16)
    partial_value = jnp.dot(rotated, down_weight[0], preferred_element_type=jnp.float32)
    summed = lax.psum_scatter(partial_value, "tensor", scatter_dimension=1, tiled=True).astype(
        jnp.bfloat16
    )
    returned = lax.all_to_all(
        summed.reshape(experts, capacity, -1), "expert", split_axis=0, concat_axis=0, tiled=True
    )
    picked = (
        returned.reshape(experts * capacity, -1)[target]
        .astype(jnp.float32)
        .reshape(tok_rows, top_count, -1)
    )
    route = route_weights.astype(jnp.float32)
    route = route / jnp.sum(route, axis=1, keepdims=True)
    return jnp.sum(picked * route[:, :, None], axis=1).astype(jnp.bfloat16)


def shards(*arrays):
    experts = lax.axis_size("expert")
    top = arrays[2].shape[1]
    dense = 2 * top >= experts and experts % 4 == 0 and experts & (experts - 1) == 0
    return (every_expert if dense else chosen_experts)(*arrays)


def solution(mesh):
    return jax.shard_map(
        shards,
        mesh=mesh,
        in_specs=(
            P(("replica", "expert"), "tensor"),
            P(("replica", "expert"), "tensor"),
            P(("replica", "expert"), None),
            P(("replica", "expert"), None),
            P("expert", None, "tensor"),
            P("expert", None, "tensor"),
            P("expert", "tensor", None),
        ),
        out_specs=P(("replica", "expert"), "tensor"),
        check_vma=False,
    )
```

```python
import functools
import math

import jax
import jax.numpy as jnp
from jax import lax
from jax.experimental import pallas as pl
from jax.experimental.pallas import tpu as pltpu
from jax.sharding import PartitionSpec as P

WALSH = 128
LANES = 128
VMEM_BYTES = 8 << 20


def walsh_signs(length):
    indices = jnp.arange(length, dtype=jnp.int32)
    parity = jnp.zeros((length, length), jnp.int32)
    for bit_index in range(length.bit_length() - 1):
        parity = parity + jnp.bitwise_and(
            jnp.bitwise_and(
                jnp.right_shift(indices[:, None], bit_index),
                jnp.right_shift(indices[None, :], bit_index),
            ),
            1,
        )
    return (1 - 2 * (parity % 2)).astype(jnp.float32)


def swap(array, masks, core=0):
    experts = lax.axis_size("expert")
    pairs = [
        (e * 2 + t, (e ^ masks[t]) * 2 + (t ^ core)) for e in range(experts) for t in range(2)
    ]
    return lax.ppermute(array, ("expert", "tensor"), pairs)


def cost():
    return pl.CostEstimate(flops=10**9, bytes_accessed=10**6, transcendentals=0)


def scaled_tokens(values, scales, ids, route_weights, experts):
    rows, features = values.shape
    blocks, top = scales.shape[1], ids.shape[1]
    width = features // blocks

    def kernel(values_ref, scales_ref, ids_ref, weights_ref, out_ref):
        spread = (
            lax.broadcasted_iota(jnp.int32, (blocks, features), 1) // width
            == lax.broadcasted_iota(jnp.int32, (blocks, features), 0)
        )
        factor = lax.dot_general(
            scales_ref[...],
            jnp.where(spread, 1.0, 0.0).astype(jnp.bfloat16),
            (((0,), (0,)), ((), ())),
            preferred_element_type=jnp.float32,
        )
        out_ref[:, :features] = (values_ref[...].astype(jnp.float32) * factor).astype(jnp.bfloat16)
        weights = weights_ref[...].astype(jnp.float32)
        route = weights / jnp.sum(weights, axis=0, keepdims=True)
        lane = lax.broadcasted_iota(jnp.int32, (LANES, rows), 0)
        expert = lax.rem(lane, experts)
        table = jnp.zeros((LANES, rows), jnp.float32)
        for k in range(top):
            table = table + jnp.where(ids_ref[k : k + 1, :] == expert, route[k : k + 1, :], 0.0)
        high = table.astype(jnp.bfloat16).astype(jnp.float32)
        tail = jnp.where(lane < experts, high, jnp.where(lane < 2 * experts, table - high, 0.0))
        same = lax.broadcasted_iota(jnp.int32, (rows, rows), 0) == lax.broadcasted_iota(
            jnp.int32, (rows, rows), 1
        )
        out_ref[:, features:] = lax.dot_general(
            jnp.where(same, 1.0, 0.0).astype(jnp.bfloat16),
            tail.astype(jnp.bfloat16),
            (((1,), (1,)), ((), ())),
            preferred_element_type=jnp.float32,
        ).astype(jnp.bfloat16)

    return pl.pallas_call(
        kernel,
        out_shape=jax.ShapeDtypeStruct((rows, features + LANES), jnp.bfloat16),
        cost_estimate=cost(),
        name="scaled_tokens",
    )(values, scales.T, ids.T, route_weights.T)


def pick_rows(near, next_near, lanes, capacity, after):
    rows, wide = near.shape
    count = 2 * capacity

    def kernel(near_ref, next_ref, lanes_ref, after_ref, mine_ref, theirs_ref, choice_ref):
        del after_ref
        both = jnp.concatenate([near_ref[...], next_ref[...]], axis=0)
        tails = jnp.concatenate([near_ref[:, wide - LANES :], next_ref[:, wide - LANES :]], axis=0)
        chosen = jnp.where(tails.astype(jnp.float32) > 0.0, 1.0, 0.0).astype(jnp.bfloat16)
        named = lax.dot_general(
            lanes_ref[...], chosen, (((1,), (1,)), ((), ())), preferred_element_type=jnp.float32
        )
        one = lax.broadcasted_iota(jnp.int32, (2 * rows, 2 * rows), 0)
        two = lax.broadcasted_iota(jnp.int32, (2 * rows, 2 * rows), 1)
        before = jnp.where((one < two) & (one // rows == two // rows), 1.0, 0.0)
        rank = jnp.dot(
            named.astype(jnp.bfloat16),
            before.astype(jnp.bfloat16),
            preferred_element_type=jnp.float32,
        )
        place = jnp.where(named > 0.5, rank, -1.0).astype(jnp.int32)
        slot = lax.broadcasted_iota(jnp.int32, (2 * count, 2 * rows), 0)
        token = lax.broadcasted_iota(jnp.int32, (2 * count, 2 * rows), 1)
        wanted = jnp.where(slot < count, place[0:1, :], place[1:2, :])
        block = lax.rem(slot, count) // capacity
        hit = (wanted == lax.rem(slot, capacity)) & (token // rows == block)
        choice = jnp.where(hit, 1.0, 0.0).astype(jnp.bfloat16)
        choice_ref[...] = choice
        picked = jnp.dot(choice, both, preferred_element_type=jnp.float32).astype(jnp.bfloat16)
        mine_ref[...] = picked[:count]
        theirs_ref[...] = picked[count:]

    vmem = pl.BlockSpec(memory_space=pltpu.VMEM)
    return pl.pallas_call(
        kernel,
        in_specs=[vmem, vmem, vmem, pl.BlockSpec(memory_space=pl.ANY)],
        out_shape=[
            jax.ShapeDtypeStruct((count, wide), jnp.bfloat16),
            jax.ShapeDtypeStruct((count, wide), jnp.bfloat16),
            jax.ShapeDtypeStruct((2 * count, 2 * rows), jnp.bfloat16),
        ],
        compiler_params=pltpu.CompilerParams(vmem_limit_bytes=VMEM_BYTES),
        cost_estimate=cost(),
        name="pick_rows",
    )(near, next_near, lanes, after)


def in_this_order(product, block):
    return jnp.concatenate(
        [
            product[:block],
            product[2 * block : 3 * block],
            product[block : 2 * block],
            product[3 * block :],
        ],
        axis=0,
    )


def hidden_units(core, near, near_pair, far, far_pair, gate, up, after):
    count = near.shape[0]
    rows = 2 * count
    features, units = gate.shape
    half = features // 2
    step = LANES

    def kernel(core_ref, near_ref, near_pair_ref, far_ref, far_pair_ref, gate_ref, up_ref,
               after_ref, out_ref, own_rows, other_rows):
        del after_ref
        own_rows[:count] = near_ref[:, :half]
        own_rows[count:] = far_ref[:, :half]
        other_rows[:count] = near_pair_ref[:, :half]
        other_rows[count:] = far_pair_ref[:, :half]
        own = pl.multiple_of(core_ref[0] * half, half)
        other = pl.multiple_of((1 - core_ref[0]) * half, half)
        for at in range(0, units, step):
            cols = slice(at, at + step)
            w_own = jnp.concatenate(
                [gate_ref[pl.ds(own, half), cols], up_ref[pl.ds(own, half), cols]], axis=1
            )
            w_other = jnp.concatenate(
                [gate_ref[pl.ds(other, half), cols], up_ref[pl.ds(other, half), cols]], axis=1
            )
            both = jnp.dot(
                own_rows[...], w_own, preferred_element_type=jnp.float32
            ) + in_this_order(
                jnp.dot(other_rows[...], w_other, preferred_element_type=jnp.float32), count // 2
            )
            gate_out, up_out = both[:, :step], both[:, step:]
            out_ref[:, cols] = (gate_out / (1.0 + jnp.exp(-gate_out)) * up_out).astype(jnp.bfloat16)

    vmem = pl.BlockSpec(memory_space=pltpu.VMEM)
    return pl.pallas_call(
        kernel,
        in_specs=[pl.BlockSpec(memory_space=pltpu.SMEM)]
        + [vmem] * 6
        + [pl.BlockSpec(memory_space=pl.ANY)],
        scratch_shapes=[pltpu.VMEM((rows, half), jnp.bfloat16)] * 2,
        out_shape=jax.ShapeDtypeStruct((rows, units), jnp.bfloat16),
        compiler_params=pltpu.CompilerParams(vmem_limit_bytes=VMEM_BYTES),
        cost_estimate=cost(),
        name="hidden_units",
    )(core, near, near_pair, far, far_pair, gate, up, after)


def routed_outputs(core, mine, theirs, mix, down, down_pair, near, far, lanes, after):
    rows, units = mine.shape
    features = down.shape[1] // 2
    groups = units // WALSH
    count = rows // 2
    step = min(512, features)

    def kernel(core_ref, mine_ref, theirs_ref, mix_ref, down_ref, pair_ref, near_ref, far_ref,
               lanes_ref, after_ref, near_out, far_out, turned):
        del after_ref
        for g in range(groups):
            cols = slice(g * WALSH, (g + 1) * WALSH)
            both = jnp.dot(
                mine_ref[:, cols], mix_ref[:WALSH], preferred_element_type=jnp.float32
            ) + in_this_order(
                jnp.dot(theirs_ref[:, cols], mix_ref[WALSH:], preferred_element_type=jnp.float32),
                count // 2,
            )
            both = both.astype(jnp.bfloat16)
            turned[:, cols] = both[:, :WALSH]
            turned[:, units + g * WALSH : units + (g + 1) * WALSH] = both[:, WALSH:]
        tails = jnp.concatenate([near_ref[:, features:], far_ref[:, features:]], axis=0)
        route = jnp.sum(tails.astype(jnp.float32) * lanes_ref[...], axis=1, keepdims=True)
        for at in range(0, features, step):
            cols = pl.ds(pl.multiple_of(core_ref[0] * features + at, step), step)
            out = jnp.dot(
                turned[:, :units], down_ref[:, cols], preferred_element_type=jnp.float32
            ) + jnp.dot(turned[:, units:], pair_ref[:, cols], preferred_element_type=jnp.float32)
            scaled = (out * route).astype(jnp.bfloat16)
            near_out[:, at : at + step] = scaled[:count]
            far_out[:, at : at + step] = scaled[count:]

    vmem = pl.BlockSpec(memory_space=pltpu.VMEM)
    return pl.pallas_call(
        kernel,
        in_specs=[pl.BlockSpec(memory_space=pltpu.SMEM)]
        + [vmem] * 8
        + [pl.BlockSpec(memory_space=pl.ANY)],
        scratch_shapes=[pltpu.VMEM((rows, 2 * units), jnp.bfloat16)],
        out_shape=[
            jax.ShapeDtypeStruct((count, features), jnp.bfloat16),
            jax.ShapeDtypeStruct((count, features), jnp.bfloat16),
        ],
        compiler_params=pltpu.CompilerParams(vmem_limit_bytes=VMEM_BYTES),
        cost_estimate=cost(),
        name="routed_outputs",
    )(core, mine, theirs, mix, down, down_pair, near, far, lanes, after)


def spread_rows(choice, mine, back, after):
    count, features = mine.shape
    rows = choice.shape[1] // 2

    def kernel(choice_ref, mine_ref, back_ref, after_ref, keep_ref, send_ref):
        del after_ref
        both = lax.dot_general(
            choice_ref[...],
            jnp.concatenate([mine_ref[...], back_ref[...]], axis=0),
            (((0,), (0,)), ((), ())),
            preferred_element_type=jnp.float32,
        )
        keep_ref[...] = both[:rows]
        send_ref[...] = both[rows:].astype(jnp.bfloat16)

    vmem = pl.BlockSpec(memory_space=pltpu.VMEM)
    return pl.pallas_call(
        kernel,
        in_specs=[vmem, vmem, vmem, pl.BlockSpec(memory_space=pl.ANY)],
        out_shape=[
            jax.ShapeDtypeStruct((rows, features), jnp.float32),
            jax.ShapeDtypeStruct((rows, features), jnp.bfloat16),
        ],
        compiler_params=pltpu.CompilerParams(vmem_limit_bytes=VMEM_BYTES),
        cost_estimate=cost(),
        name="spread_rows",
    )(choice, mine, back, after)


def add_rows(parts, kind, after):
    def kernel(*refs):
        total = refs[0][...].astype(jnp.float32)
        for ref in refs[1 : len(parts)]:
            total = total + ref[...].astype(jnp.float32)
        refs[-1][...] = total.astype(kind)

    vmem = pl.BlockSpec(memory_space=pltpu.VMEM)
    return pl.pallas_call(
        kernel,
        in_specs=[vmem] * len(parts) + [pl.BlockSpec(memory_space=pl.ANY)],
        out_shape=jax.ShapeDtypeStruct(parts[0].shape, kind),
        compiler_params=pltpu.CompilerParams(vmem_limit_bytes=VMEM_BYTES),
        cost_estimate=cost(),
        name="add_rows",
    )(*parts, after)


def every_expert(
    token_values, token_scales, expert_ids, route_weights, gate_weight, up_weight, down_weight
):
    experts = lax.axis_size("expert")
    core_index = lax.axis_index("tensor")
    core = core_index.astype(jnp.int32).reshape(1)
    expert = lax.axis_index("expert")
    rows, features = token_values.shape
    top = expert_ids.shape[1]
    capacity = min(rows, 5 * rows * top // (4 * experts))
    gate, up, down = gate_weight[0], up_weight[0], down_weight[0]
    first, second = (1, 2), (2, 1)
    line = experts // 4

    block = scaled_tokens(token_values, token_scales, expert_ids, route_weights, experts)
    blocks = [block]
    for index in range(1, line):
        if index % 2 == 1 and index > 1:
            blocks.append(swap(blocks[index - 1], (4, 4)))
        else:
            blocks.append(swap(block, (4 * index, 4 * index)))

    down_pair = swap(down, (0, 0), 1)

    signs = walsh_signs(WALSH) / math.sqrt(2 * WALSH)
    sign = jnp.where(core_index == 0, 1.0, -1.0)
    mix = jnp.concatenate(
        [
            jnp.concatenate([signs * sign, signs], axis=1),
            jnp.concatenate([signs, -signs * sign], axis=1),
        ],
        axis=0,
    ).astype(jnp.bfloat16)
    lane = jnp.arange(LANES, dtype=jnp.int32)[None, :]
    lanes = ((lane % experts == expert) & (lane < 2 * experts)).astype(jnp.float32)
    beyond = expert ^ jnp.where(core_index == 0, second[0], second[1])
    named = jnp.concatenate([lane == expert, lane == beyond] + [lane < 0] * 6, axis=0).astype(
        jnp.bfloat16
    )

    state = [dict() for _ in range(line)]
    last = blocks[-2]
    total = None

    def pick(k):
        nonlocal last
        it = state[k]
        it["mine"], away, it["choice"] = pick_rows(
            blocks[k], swap(blocks[k], first), named, capacity, last
        )
        it["mine_pair"] = swap(it["mine"], (0, 0), 1)
        it["far"] = swap(away, second)
        it["far_pair"] = swap(it["far"], (0, 0), 1)
        last = it["choice"]

    def expand_units(k):
        nonlocal last
        it = state[k]
        it["hidden"] = hidden_units(
            core, it["mine"], it["mine_pair"], it["far"], it["far_pair"], gate, up, last
        )
        it["hidden_pair"] = swap(it["hidden"], (0, 0), 1)
        last = it["hidden"]

    def contract_units(k):
        nonlocal last
        it = state[k]
        it["out"], away = routed_outputs(
            core, it["hidden"], it["hidden_pair"], mix, down, down_pair, it["mine"], it["far"],
            lanes, last,
        )
        it["back"] = swap(away, second)
        last = it["out"]

    def spread(k):
        nonlocal last
        it = state[k]
        it["keep"], away = spread_rows(it["choice"], it["out"], it["back"], last)
        it["next"] = swap(away, first)
        last = it["keep"]

    def settle(k):
        nonlocal last, total
        it = state[k]
        if k == 0:
            total = last = add_rows([it["keep"], it["next"]], jnp.float32, last)
            return
        parts = [it["keep"], it["next"]]
        if k % 2 == 1 and k > 1:
            parts.append(state[k - 1]["sent"])
        last = add_rows(parts, jnp.bfloat16, last)
        mask = 4 if k % 2 == 0 else 4 * k
        it["sent"] = swap(last, (mask, mask))

    def absorb(k):
        nonlocal last, total
        if k % 2 == 1:
            kind = jnp.bfloat16 if k == line - 1 else jnp.float32
            total = last = add_rows([total, state[k]["sent"]], kind, last)

    near_round = lambda k: (0, 1, 1, 2)[min(k, 3)] + max(0, k - 3)
    stages = (
        (settle, lambda k: 6 + near_round(k)),
        (absorb, lambda k: 7 + near_round(k)),
        (spread, lambda k: 5 + near_round(k)),
        (contract_units, lambda k: 4 + near_round(k)),
        (expand_units, lambda k: 3 + near_round(k)),
        (pick, lambda k: 1 + near_round(k) - (k > 2) / 2),
    )
    due = [(when(k), name, k) for k in range(line) for name, (_, when) in enumerate(stages)]
    for _, name, k in sorted(due):
        stages[name][0](k)
    return total


def chosen_experts(
    token_values, token_scales, expert_ids, route_weights, gate_weight, up_weight, down_weight
):
    tok_rows, top_count = expert_ids.shape
    experts = lax.axis_size("expert")
    capacity = min(tok_rows, 5 * tok_rows * top_count // (4 * experts))
    flat_ids = expert_ids.reshape(-1)
    onehot = (flat_ids[:, None] == jnp.arange(experts, dtype=jnp.int32)[None, :]).astype(jnp.int32)
    slot_index = jnp.sum(jnp.cumsum(onehot, axis=0) * onehot, axis=1) - 1
    target = flat_ids * capacity + slot_index
    owner_token = jnp.arange(tok_rows * top_count, dtype=jnp.int32) // top_count
    source = jnp.full((experts * capacity,), tok_rows, jnp.int32).at[target].set(owner_token)
    padded_values = jnp.concatenate(
        [token_values, jnp.zeros((1, token_values.shape[1]), token_values.dtype)], axis=0
    )
    padded_scales = jnp.concatenate(
        [token_scales, jnp.zeros((1, token_scales.shape[1]), token_scales.dtype)], axis=0
    )
    send_values = padded_values[source].reshape(experts, capacity, -1)
    send_scales = padded_scales[source].reshape(experts, capacity, -1)
    arrived_values, arrived_scales = (
        lax.all_to_all(send_values, "expert", split_axis=0, concat_axis=0, tiled=True),
        lax.all_to_all(send_scales, "expert", split_axis=0, concat_axis=0, tiled=True),
    )
    joined_values, joined_scales = (
        lax.all_gather(arrived_values, "tensor", axis=2, tiled=True),
        lax.all_gather(arrived_scales, "tensor", axis=2, tiled=True),
    )
    row_count = experts * capacity
    feature_count = joined_values.shape[2]
    scale_count = joined_scales.shape[2]
    dequant = (
        (
            joined_values.astype(jnp.float32).reshape(
                row_count, scale_count, feature_count // scale_count
            )
            * joined_scales.astype(jnp.float32).reshape(row_count, scale_count, 1)
        )
        .reshape(row_count, feature_count)
        .astype(jnp.bfloat16)
    )
    gate_out = jnp.dot(dequant, gate_weight[0], preferred_element_type=jnp.float32)
    up_out = jnp.dot(dequant, up_weight[0], preferred_element_type=jnp.float32)
    hidden = (jax.nn.silu(gate_out) * up_out).astype(jnp.bfloat16)
    partner = swap(hidden, (0, 0), 1)
    own_part = hidden.astype(jnp.float32)
    theirs = partner.astype(jnp.float32)
    combined = jnp.where(lax.axis_index("tensor") == 0, own_part + theirs, theirs - own_part)
    groups = hidden.shape[1] // WALSH
    norm_factor = 1.0 / math.sqrt(2 * WALSH)
    turned = (
        jnp.einsum(
            "rgj,kj->rgk",
            combined.reshape(row_count, groups, WALSH),
            walsh_signs(WALSH),
            precision=lax.Precision.HIGHEST,
        )
        * norm_factor
    )
    rotated = turned.reshape(row_count, -1).astype(jnp.bfloat16)
    partial_value = jnp.dot(rotated, down_weight[0], preferred_element_type=jnp.float32)
    summed = lax.psum_scatter(partial_value, "tensor", scatter_dimension=1, tiled=True).astype(
        jnp.bfloat16
    )
    returned = lax.all_to_all(
        summed.reshape(experts, capacity, -1), "expert", split_axis=0, concat_axis=0, tiled=True
    )
    picked = (
        returned.reshape(experts * capacity, -1)[target]
        .astype(jnp.float32)
        .reshape(tok_rows, top_count, -1)
    )
    route = route_weights.astype(jnp.float32)
    route = route / jnp.sum(route, axis=1, keepdims=True)
    return jnp.sum(picked * route[:, :, None], axis=1).astype(jnp.bfloat16)


def shards(*arrays):
    experts = lax.axis_size("expert")
    top = arrays[2].shape[1]
    dense = 2 * top >= experts and experts % 4 == 0 and experts & (experts - 1) == 0
    return (every_expert if dense else chosen_experts)(*arrays)


def solution(mesh):
    return jax.shard_map(
        shards,
        mesh=mesh,
        in_specs=(
            P(("replica", "expert"), "tensor"),
            P(("replica", "expert"), "tensor"),
            P(("replica", "expert"), None),
            P(("replica", "expert"), None),
            P("expert", None, "tensor"),
            P("expert", None, "tensor"),
            P("expert", "tensor", None),
        ),
        out_specs=P(("replica", "expert"), "tensor"),
        check_vma=False,
    )
```

```python
import functools
import math

import jax
import jax.numpy as jnp
from jax import lax
from jax.experimental import pallas as pl
from jax.experimental.pallas import tpu as pltpu
from jax.sharding import PartitionSpec as P

WALSH = 128
LANES = 128
ORDER = (
    (0, 1, 2, 3),
    (4, 6, 7, 8),
    (5, 10, 9, 11),
    (12, 14, 13, 15),
    (19, 17, 16, 18),
    (19.1, 20, 16.1, 21),
)
HEAVY, LIGHT = 2 * 10**9, 10**7
VMEM_BYTES = 8 << 20


def walsh_signs(length):
    indices = jnp.arange(length, dtype=jnp.int32)
    parity = jnp.zeros((length, length), jnp.int32)
    for bit_index in range(length.bit_length() - 1):
        parity = parity + jnp.bitwise_and(
            jnp.bitwise_and(
                jnp.right_shift(indices[:, None], bit_index),
                jnp.right_shift(indices[None, :], bit_index),
            ),
            1,
        )
    return (1 - 2 * (parity % 2)).astype(jnp.float32)


def swap(array, masks, core=0):
    experts = lax.axis_size("expert")
    pairs = [
        (e * 2 + t, (e ^ masks[t]) * 2 + (t ^ core)) for e in range(experts) for t in range(2)
    ]
    return lax.ppermute(array, ("expert", "tensor"), pairs)


def cost(flops=HEAVY):
    return pl.CostEstimate(flops=flops, bytes_accessed=10**6, transcendentals=0)


def scaled_tokens(values, scales, ids, route_weights, experts):
    rows, features = values.shape
    blocks, top = scales.shape[1], ids.shape[1]
    width = features // blocks

    def kernel(values_ref, scales_ref, ids_ref, weights_ref, out_ref):
        spread = (
            lax.broadcasted_iota(jnp.int32, (blocks, features), 1) // width
            == lax.broadcasted_iota(jnp.int32, (blocks, features), 0)
        )
        factor = lax.dot_general(
            scales_ref[...],
            jnp.where(spread, 1.0, 0.0).astype(jnp.bfloat16),
            (((0,), (0,)), ((), ())),
            preferred_element_type=jnp.float32,
        )
        out_ref[:, :features] = (values_ref[...].astype(jnp.float32) * factor).astype(jnp.bfloat16)
        weights = weights_ref[...].astype(jnp.float32)
        route = weights / jnp.sum(weights, axis=0, keepdims=True)
        lane = lax.broadcasted_iota(jnp.int32, (LANES, rows), 0)
        expert = lax.rem(lane, experts)
        table = jnp.zeros((LANES, rows), jnp.float32)
        for k in range(top):
            table = table + jnp.where(ids_ref[k : k + 1, :] == expert, route[k : k + 1, :], 0.0)
        high = table.astype(jnp.bfloat16).astype(jnp.float32)
        tail = jnp.where(lane < experts, high, jnp.where(lane < 2 * experts, table - high, 0.0))
        same = lax.broadcasted_iota(jnp.int32, (rows, rows), 0) == lax.broadcasted_iota(
            jnp.int32, (rows, rows), 1
        )
        out_ref[:, features:] = lax.dot_general(
            jnp.where(same, 1.0, 0.0).astype(jnp.bfloat16),
            tail.astype(jnp.bfloat16),
            (((1,), (1,)), ((), ())),
            preferred_element_type=jnp.float32,
        ).astype(jnp.bfloat16)

    return pl.pallas_call(
        kernel,
        out_shape=jax.ShapeDtypeStruct((rows, features + LANES), jnp.bfloat16),
        cost_estimate=cost(),
        name="scaled_tokens",
    )(values, scales.T, ids.T, route_weights.T)


def pick_rows(near, next_near, lanes, capacity, after):
    rows, wide = near.shape
    count = 2 * capacity

    def kernel(near_ref, next_ref, lanes_ref, after_ref, mine_ref, theirs_ref, choice_ref):
        del after_ref
        both = jnp.concatenate([near_ref[...], next_ref[...]], axis=0)
        tails = jnp.concatenate([near_ref[:, wide - LANES :], next_ref[:, wide - LANES :]], axis=0)
        chosen = jnp.where(tails.astype(jnp.float32) > 0.0, 1.0, 0.0).astype(jnp.bfloat16)
        named = lax.dot_general(
            lanes_ref[...], chosen, (((1,), (1,)), ((), ())), preferred_element_type=jnp.float32
        )
        one = lax.broadcasted_iota(jnp.int32, (2 * rows, 2 * rows), 0)
        two = lax.broadcasted_iota(jnp.int32, (2 * rows, 2 * rows), 1)
        before = jnp.where((one < two) & (one // rows == two // rows), 1.0, 0.0)
        rank = jnp.dot(
            named.astype(jnp.bfloat16),
            before.astype(jnp.bfloat16),
            preferred_element_type=jnp.float32,
        )
        place = jnp.where(named > 0.5, rank, -1.0).astype(jnp.int32)
        slot = lax.broadcasted_iota(jnp.int32, (2 * count, 2 * rows), 0)
        token = lax.broadcasted_iota(jnp.int32, (2 * count, 2 * rows), 1)
        wanted = jnp.where(slot < count, place[0:1, :], place[1:2, :])
        block = lax.rem(slot, count) // capacity
        hit = (wanted == lax.rem(slot, capacity)) & (token // rows == block)
        choice = jnp.where(hit, 1.0, 0.0).astype(jnp.bfloat16)
        choice_ref[...] = choice
        picked = jnp.dot(choice, both, preferred_element_type=jnp.float32).astype(jnp.bfloat16)
        mine_ref[...] = picked[:count]
        theirs_ref[...] = picked[count:]

    vmem = pl.BlockSpec(memory_space=pltpu.VMEM)
    return pl.pallas_call(
        kernel,
        in_specs=[vmem, vmem, vmem, pl.BlockSpec(memory_space=pl.ANY)],
        out_shape=[
            jax.ShapeDtypeStruct((count, wide), jnp.bfloat16),
            jax.ShapeDtypeStruct((count, wide), jnp.bfloat16),
            jax.ShapeDtypeStruct((2 * count, 2 * rows), jnp.bfloat16),
        ],
        compiler_params=pltpu.CompilerParams(vmem_limit_bytes=VMEM_BYTES),
        cost_estimate=cost(),
        name="pick_rows",
    )(near, next_near, lanes, after)


def in_this_order(product, block):
    return jnp.concatenate(
        [
            product[:block],
            product[2 * block : 3 * block],
            product[block : 2 * block],
            product[3 * block :],
        ],
        axis=0,
    )


def hidden_units(core, near, near_pair, far, far_pair, gate, up, after):
    count = near.shape[0]
    rows = 2 * count
    features, units = gate.shape
    half = features // 2
    step = LANES

    def kernel(core_ref, near_ref, near_pair_ref, far_ref, far_pair_ref, gate_ref, up_ref,
               after_ref, out_ref, own_rows, other_rows):
        del after_ref
        own_rows[:count] = near_ref[:, :half]
        own_rows[count:] = far_ref[:, :half]
        other_rows[:count] = near_pair_ref[:, :half]
        other_rows[count:] = far_pair_ref[:, :half]
        own = pl.multiple_of(core_ref[0] * half, half)
        other = pl.multiple_of((1 - core_ref[0]) * half, half)
        for at in range(0, units, step):
            cols = slice(at, at + step)
            w_own = jnp.concatenate(
                [gate_ref[pl.ds(own, half), cols], up_ref[pl.ds(own, half), cols]], axis=1
            )
            w_other = jnp.concatenate(
                [gate_ref[pl.ds(other, half), cols], up_ref[pl.ds(other, half), cols]], axis=1
            )
            both = jnp.dot(
                own_rows[...], w_own, preferred_element_type=jnp.float32
            ) + in_this_order(
                jnp.dot(other_rows[...], w_other, preferred_element_type=jnp.float32), count // 2
            )
            gate_out, up_out = both[:, :step], both[:, step:]
            out_ref[:, cols] = (gate_out / (1.0 + jnp.exp(-gate_out)) * up_out).astype(jnp.bfloat16)

    vmem = pl.BlockSpec(memory_space=pltpu.VMEM)
    return pl.pallas_call(
        kernel,
        in_specs=[pl.BlockSpec(memory_space=pltpu.SMEM)]
        + [vmem] * 6
        + [pl.BlockSpec(memory_space=pl.ANY)],
        scratch_shapes=[pltpu.VMEM((rows, half), jnp.bfloat16)] * 2,
        out_shape=jax.ShapeDtypeStruct((rows, units), jnp.bfloat16),
        compiler_params=pltpu.CompilerParams(vmem_limit_bytes=VMEM_BYTES),
        cost_estimate=cost(),
        name="hidden_units",
    )(core, near, near_pair, far, far_pair, gate, up, after)


def routed_outputs(core, mine, theirs, mix, down, down_pair, near, far, lanes, after):
    rows, units = mine.shape
    features = down.shape[1] // 2
    groups = units // WALSH
    count = rows // 2
    step = min(512, features)

    def kernel(core_ref, mine_ref, theirs_ref, mix_ref, down_ref, pair_ref, near_ref, far_ref,
               lanes_ref, after_ref, near_out, far_out, turned):
        del after_ref
        for g in range(groups):
            cols = slice(g * WALSH, (g + 1) * WALSH)
            both = jnp.dot(
                mine_ref[:, cols], mix_ref[:WALSH], preferred_element_type=jnp.float32
            ) + in_this_order(
                jnp.dot(theirs_ref[:, cols], mix_ref[WALSH:], preferred_element_type=jnp.float32),
                count // 2,
            )
            both = both.astype(jnp.bfloat16)
            turned[:, cols] = both[:, :WALSH]
            turned[:, units + g * WALSH : units + (g + 1) * WALSH] = both[:, WALSH:]
        tails = jnp.concatenate([near_ref[:, features:], far_ref[:, features:]], axis=0)
        route = jnp.sum(tails.astype(jnp.float32) * lanes_ref[...], axis=1, keepdims=True)
        for at in range(0, features, step):
            cols = pl.ds(pl.multiple_of(core_ref[0] * features + at, step), step)
            out = jnp.dot(
                turned[:, :units], down_ref[:, cols], preferred_element_type=jnp.float32
            ) + jnp.dot(turned[:, units:], pair_ref[:, cols], preferred_element_type=jnp.float32)
            scaled = (out * route).astype(jnp.bfloat16)
            near_out[:, at : at + step] = scaled[:count]
            far_out[:, at : at + step] = scaled[count:]

    vmem = pl.BlockSpec(memory_space=pltpu.VMEM)
    return pl.pallas_call(
        kernel,
        in_specs=[pl.BlockSpec(memory_space=pltpu.SMEM)]
        + [vmem] * 8
        + [pl.BlockSpec(memory_space=pl.ANY)],
        scratch_shapes=[pltpu.VMEM((rows, 2 * units), jnp.bfloat16)],
        out_shape=[
            jax.ShapeDtypeStruct((count, features), jnp.bfloat16),
            jax.ShapeDtypeStruct((count, features), jnp.bfloat16),
        ],
        compiler_params=pltpu.CompilerParams(vmem_limit_bytes=VMEM_BYTES),
        cost_estimate=cost(),
        name="routed_outputs",
    )(core, mine, theirs, mix, down, down_pair, near, far, lanes, after)


def spread_rows(choice, mine, back, after):
    count, features = mine.shape
    rows = choice.shape[1] // 2

    def kernel(choice_ref, mine_ref, back_ref, after_ref, keep_ref, send_ref):
        del after_ref
        both = lax.dot_general(
            choice_ref[...],
            jnp.concatenate([mine_ref[...], back_ref[...]], axis=0),
            (((0,), (0,)), ((), ())),
            preferred_element_type=jnp.float32,
        )
        keep_ref[...] = both[:rows]
        send_ref[...] = both[rows:].astype(jnp.bfloat16)

    vmem = pl.BlockSpec(memory_space=pltpu.VMEM)
    return pl.pallas_call(
        kernel,
        in_specs=[vmem, vmem, vmem, pl.BlockSpec(memory_space=pl.ANY)],
        out_shape=[
            jax.ShapeDtypeStruct((rows, features), jnp.float32),
            jax.ShapeDtypeStruct((rows, features), jnp.bfloat16),
        ],
        compiler_params=pltpu.CompilerParams(vmem_limit_bytes=VMEM_BYTES),
        cost_estimate=cost(),
        name="spread_rows",
    )(choice, mine, back, after)


def add_rows(parts, kind, after):
    def kernel(*refs):
        total = refs[0][...].astype(jnp.float32)
        for ref in refs[1 : len(parts)]:
            total = total + ref[...].astype(jnp.float32)
        refs[-1][...] = total.astype(kind)

    vmem = pl.BlockSpec(memory_space=pltpu.VMEM)
    return pl.pallas_call(
        kernel,
        in_specs=[vmem] * len(parts) + [pl.BlockSpec(memory_space=pl.ANY)],
        out_shape=jax.ShapeDtypeStruct(parts[0].shape, kind),
        compiler_params=pltpu.CompilerParams(vmem_limit_bytes=VMEM_BYTES),
        cost_estimate=cost(LIGHT),
        name="add_rows",
    )(*parts, after)


def every_expert(
    token_values, token_scales, expert_ids, route_weights, gate_weight, up_weight, down_weight
):
    experts = lax.axis_size("expert")
    core_index = lax.axis_index("tensor")
    core = core_index.astype(jnp.int32).reshape(1)
    expert = lax.axis_index("expert")
    rows, features = token_values.shape
    top = expert_ids.shape[1]
    capacity = min(rows, 5 * rows * top // (4 * experts))
    gate, up, down = gate_weight[0], up_weight[0], down_weight[0]
    first, second = (1, 2), (2, 1)
    line = experts // 4

    block = scaled_tokens(token_values, token_scales, expert_ids, route_weights, experts)
    blocks = [block]
    for index in range(1, line):
        if index % 2 == 1 and index > 1:
            blocks.append(swap(blocks[index - 1], (4, 4)))
        else:
            blocks.append(swap(block, (4 * index, 4 * index)))

    down_pair = swap(down, (0, 0), 1)

    signs = walsh_signs(WALSH) / math.sqrt(2 * WALSH)
    sign = jnp.where(core_index == 0, 1.0, -1.0)
    mix = jnp.concatenate(
        [
            jnp.concatenate([signs * sign, signs], axis=1),
            jnp.concatenate([signs, -signs * sign], axis=1),
        ],
        axis=0,
    ).astype(jnp.bfloat16)
    lane = jnp.arange(LANES, dtype=jnp.int32)[None, :]
    lanes = ((lane % experts == expert) & (lane < 2 * experts)).astype(jnp.float32)
    beyond = expert ^ jnp.where(core_index == 0, second[0], second[1])
    named = jnp.concatenate([lane == expert, lane == beyond] + [lane < 0] * 6, axis=0).astype(
        jnp.bfloat16
    )

    state = [dict() for _ in range(line)]
    last = named
    total = None

    def pick(k):
        nonlocal last
        it = state[k]
        it["mine"], away, it["choice"] = pick_rows(
            blocks[k], swap(blocks[k], first), named, capacity, last
        )
        it["mine_pair"] = swap(it["mine"], (0, 0), 1)
        it["far"] = swap(away, second)
        it["far_pair"] = swap(it["far"], (0, 0), 1)
        last = it["choice"]

    def expand_units(k):
        nonlocal last
        it = state[k]
        it["hidden"] = hidden_units(
            core, it["mine"], it["mine_pair"], it["far"], it["far_pair"], gate, up, last
        )
        it["hidden_pair"] = swap(it["hidden"], (0, 0), 1)
        last = it["hidden"]

    def contract_units(k):
        nonlocal last
        it = state[k]
        it["out"], away = routed_outputs(
            core, it["hidden"], it["hidden_pair"], mix, down, down_pair, it["mine"], it["far"],
            lanes, last,
        )
        it["back"] = swap(away, second)
        last = it["out"]

    def spread(k):
        nonlocal last
        it = state[k]
        it["keep"], away = spread_rows(it["choice"], it["out"], it["back"], last)
        it["next"] = swap(away, first)
        last = it["keep"]

    def settle(k):
        nonlocal last, total
        it = state[k]
        if k == 0:
            total = last = add_rows([it["keep"], it["next"]], jnp.float32, last)
            return
        parts = [it["keep"], it["next"]]
        if k % 2 == 1 and k > 1:
            parts.append(state[k - 1]["sent"])
        last = add_rows(parts, jnp.bfloat16, last)
        mask = 4 if k % 2 == 0 else 4 * k
        it["sent"] = swap(last, (mask, mask))

    def absorb(k):
        nonlocal last, total
        if k % 2 == 1:
            kind = jnp.bfloat16 if k == line - 1 else jnp.float32
            total = last = add_rows([total, state[k]["sent"]], kind, last)

    steps = (pick, expand_units, contract_units, spread, settle, absorb)
    due = [
        (times[min(k, 3)] + 10 * max(0, k - 3), name, k)
        for name, times in enumerate(ORDER)
        for k in range(line)
    ]
    for _, name, k in sorted(due):
        steps[name](k)
    return total


def chosen_experts(
    token_values, token_scales, expert_ids, route_weights, gate_weight, up_weight, down_weight
):
    tok_rows, top_count = expert_ids.shape
    experts = lax.axis_size("expert")
    capacity = min(tok_rows, 5 * tok_rows * top_count // (4 * experts))
    flat_ids = expert_ids.reshape(-1)
    onehot = (flat_ids[:, None] == jnp.arange(experts, dtype=jnp.int32)[None, :]).astype(jnp.int32)
    slot_index = jnp.sum(jnp.cumsum(onehot, axis=0) * onehot, axis=1) - 1
    target = flat_ids * capacity + slot_index
    owner_token = jnp.arange(tok_rows * top_count, dtype=jnp.int32) // top_count
    source = jnp.full((experts * capacity,), tok_rows, jnp.int32).at[target].set(owner_token)
    padded_values = jnp.concatenate(
        [token_values, jnp.zeros((1, token_values.shape[1]), token_values.dtype)], axis=0
    )
    padded_scales = jnp.concatenate(
        [token_scales, jnp.zeros((1, token_scales.shape[1]), token_scales.dtype)], axis=0
    )
    send_values = padded_values[source].reshape(experts, capacity, -1)
    send_scales = padded_scales[source].reshape(experts, capacity, -1)
    arrived_values, arrived_scales = (
        lax.all_to_all(send_values, "expert", split_axis=0, concat_axis=0, tiled=True),
        lax.all_to_all(send_scales, "expert", split_axis=0, concat_axis=0, tiled=True),
    )
    joined_values, joined_scales = (
        lax.all_gather(arrived_values, "tensor", axis=2, tiled=True),
        lax.all_gather(arrived_scales, "tensor", axis=2, tiled=True),
    )
    row_count = experts * capacity
    feature_count = joined_values.shape[2]
    scale_count = joined_scales.shape[2]
    dequant = (
        (
            joined_values.astype(jnp.float32).reshape(
                row_count, scale_count, feature_count // scale_count
            )
            * joined_scales.astype(jnp.float32).reshape(row_count, scale_count, 1)
        )
        .reshape(row_count, feature_count)
        .astype(jnp.bfloat16)
    )
    gate_out = jnp.dot(dequant, gate_weight[0], preferred_element_type=jnp.float32)
    up_out = jnp.dot(dequant, up_weight[0], preferred_element_type=jnp.float32)
    hidden = (jax.nn.silu(gate_out) * up_out).astype(jnp.bfloat16)
    partner = swap(hidden, (0, 0), 1)
    own_part = hidden.astype(jnp.float32)
    theirs = partner.astype(jnp.float32)
    combined = jnp.where(lax.axis_index("tensor") == 0, own_part + theirs, theirs - own_part)
    groups = hidden.shape[1] // WALSH
    norm_factor = 1.0 / math.sqrt(2 * WALSH)
    turned = (
        jnp.einsum(
            "rgj,kj->rgk",
            combined.reshape(row_count, groups, WALSH),
            walsh_signs(WALSH),
            precision=lax.Precision.HIGHEST,
        )
        * norm_factor
    )
    rotated = turned.reshape(row_count, -1).astype(jnp.bfloat16)
    partial_value = jnp.dot(rotated, down_weight[0], preferred_element_type=jnp.float32)
    summed = lax.psum_scatter(partial_value, "tensor", scatter_dimension=1, tiled=True).astype(
        jnp.bfloat16
    )
    returned = lax.all_to_all(
        summed.reshape(experts, capacity, -1), "expert", split_axis=0, concat_axis=0, tiled=True
    )
    picked = (
        returned.reshape(experts * capacity, -1)[target]
        .astype(jnp.float32)
        .reshape(tok_rows, top_count, -1)
    )
    route = route_weights.astype(jnp.float32)
    route = route / jnp.sum(route, axis=1, keepdims=True)
    return jnp.sum(picked * route[:, :, None], axis=1).astype(jnp.bfloat16)


def shards(*arrays):
    experts = lax.axis_size("expert")
    top = arrays[2].shape[1]
    dense = 2 * top >= experts and experts % 4 == 0 and experts & (experts - 1) == 0
    return (every_expert if dense else chosen_experts)(*arrays)


def solution(mesh):
    return jax.shard_map(
        shards,
        mesh=mesh,
        in_specs=(
            P(("replica", "expert"), "tensor"),
            P(("replica", "expert"), "tensor"),
            P(("replica", "expert"), None),
            P(("replica", "expert"), None),
            P("expert", None, "tensor"),
            P("expert", None, "tensor"),
            P("expert", "tensor", None),
        ),
        out_specs=P(("replica", "expert"), "tensor"),
        check_vma=False,
    )
```

```python
import functools
import math

import jax
import jax.numpy as jnp
from jax import lax
from jax.experimental import pallas as pl
from jax.experimental.pallas import tpu as pltpu
from jax.sharding import PartitionSpec as P

WALSH = 128
LANES = 128
ORDER = (
    (0, 1, 2, 3),
    (4, 6, 7, 8),
    (5, 10, 9, 11),
    (12, 14, 13, 16),
    (19, 17, 15, 18),
    (19.1, 20, 15.1, 21),
)
HEAVY, LIGHT = 2 * 10**9, 10**7
VMEM_BYTES = 8 << 20


def walsh_signs(length):
    indices = jnp.arange(length, dtype=jnp.int32)
    parity = jnp.zeros((length, length), jnp.int32)
    for bit_index in range(length.bit_length() - 1):
        parity = parity + jnp.bitwise_and(
            jnp.bitwise_and(
                jnp.right_shift(indices[:, None], bit_index),
                jnp.right_shift(indices[None, :], bit_index),
            ),
            1,
        )
    return (1 - 2 * (parity % 2)).astype(jnp.float32)


def swap(array, masks, core=0):
    experts = lax.axis_size("expert")
    pairs = [
        (e * 2 + t, (e ^ masks[t]) * 2 + (t ^ core)) for e in range(experts) for t in range(2)
    ]
    return lax.ppermute(array, ("expert", "tensor"), pairs)


def cost(flops=HEAVY):
    return pl.CostEstimate(flops=flops, bytes_accessed=10**6, transcendentals=0)


def scaled_tokens(values, scales, ids, route_weights, experts):
    rows, features = values.shape
    blocks, top = scales.shape[1], ids.shape[1]
    width = features // blocks

    def kernel(values_ref, scales_ref, ids_ref, weights_ref, out_ref):
        spread = (
            lax.broadcasted_iota(jnp.int32, (blocks, features), 1) // width
            == lax.broadcasted_iota(jnp.int32, (blocks, features), 0)
        )
        factor = lax.dot_general(
            scales_ref[...],
            jnp.where(spread, 1.0, 0.0).astype(jnp.bfloat16),
            (((0,), (0,)), ((), ())),
            preferred_element_type=jnp.float32,
        )
        out_ref[:, :features] = (values_ref[...].astype(jnp.float32) * factor).astype(jnp.bfloat16)
        weights = weights_ref[...].astype(jnp.float32)
        route = weights / jnp.sum(weights, axis=0, keepdims=True)
        lane = lax.broadcasted_iota(jnp.int32, (LANES, rows), 0)
        expert = lax.rem(lane, experts)
        table = jnp.zeros((LANES, rows), jnp.float32)
        for k in range(top):
            table = table + jnp.where(ids_ref[k : k + 1, :] == expert, route[k : k + 1, :], 0.0)
        high = table.astype(jnp.bfloat16).astype(jnp.float32)
        tail = jnp.where(lane < experts, high, jnp.where(lane < 2 * experts, table - high, 0.0))
        same = lax.broadcasted_iota(jnp.int32, (rows, rows), 0) == lax.broadcasted_iota(
            jnp.int32, (rows, rows), 1
        )
        out_ref[:, features:] = lax.dot_general(
            jnp.where(same, 1.0, 0.0).astype(jnp.bfloat16),
            tail.astype(jnp.bfloat16),
            (((1,), (1,)), ((), ())),
            preferred_element_type=jnp.float32,
        ).astype(jnp.bfloat16)

    return pl.pallas_call(
        kernel,
        out_shape=jax.ShapeDtypeStruct((rows, features + LANES), jnp.bfloat16),
        cost_estimate=cost(),
        name="scaled_tokens",
    )(values, scales.T, ids.T, route_weights.T)


def pick_rows(near, next_near, lanes, capacity, after):
    rows, wide = near.shape
    count = 2 * capacity

    def kernel(near_ref, next_ref, lanes_ref, after_ref, mine_ref, theirs_ref, choice_ref):
        del after_ref
        both = jnp.concatenate([near_ref[...], next_ref[...]], axis=0)
        tails = jnp.concatenate([near_ref[:, wide - LANES :], next_ref[:, wide - LANES :]], axis=0)
        chosen = jnp.where(tails.astype(jnp.float32) > 0.0, 1.0, 0.0).astype(jnp.bfloat16)
        named = lax.dot_general(
            lanes_ref[...], chosen, (((1,), (1,)), ((), ())), preferred_element_type=jnp.float32
        )
        one = lax.broadcasted_iota(jnp.int32, (2 * rows, 2 * rows), 0)
        two = lax.broadcasted_iota(jnp.int32, (2 * rows, 2 * rows), 1)
        before = jnp.where((one < two) & (one // rows == two // rows), 1.0, 0.0)
        rank = jnp.dot(
            named.astype(jnp.bfloat16),
            before.astype(jnp.bfloat16),
            preferred_element_type=jnp.float32,
        )
        place = jnp.where(named > 0.5, rank, -1.0).astype(jnp.int32)
        slot = lax.broadcasted_iota(jnp.int32, (2 * count, 2 * rows), 0)
        token = lax.broadcasted_iota(jnp.int32, (2 * count, 2 * rows), 1)
        wanted = jnp.where(slot < count, place[0:1, :], place[1:2, :])
        block = lax.rem(slot, count) // capacity
        hit = (wanted == lax.rem(slot, capacity)) & (token // rows == block)
        choice = jnp.where(hit, 1.0, 0.0).astype(jnp.bfloat16)
        choice_ref[...] = choice
        picked = jnp.dot(choice, both, preferred_element_type=jnp.float32).astype(jnp.bfloat16)
        mine_ref[...] = picked[:count]
        theirs_ref[...] = picked[count:]

    vmem = pl.BlockSpec(memory_space=pltpu.VMEM)
    return pl.pallas_call(
        kernel,
        in_specs=[vmem, vmem, vmem, pl.BlockSpec(memory_space=pl.ANY)],
        out_shape=[
            jax.ShapeDtypeStruct((count, wide), jnp.bfloat16),
            jax.ShapeDtypeStruct((count, wide), jnp.bfloat16),
            jax.ShapeDtypeStruct((2 * count, 2 * rows), jnp.bfloat16),
        ],
        compiler_params=pltpu.CompilerParams(vmem_limit_bytes=VMEM_BYTES),
        cost_estimate=cost(),
        name="pick_rows",
    )(near, next_near, lanes, after)


def in_this_order(product, block):
    return jnp.concatenate(
        [
            product[:block],
            product[2 * block : 3 * block],
            product[block : 2 * block],
            product[3 * block :],
        ],
        axis=0,
    )


def hidden_units(core, near, near_pair, far, far_pair, gate, up, after):
    count = near.shape[0]
    rows = 2 * count
    features, units = gate.shape
    half = features // 2
    step = LANES

    def kernel(core_ref, near_ref, near_pair_ref, far_ref, far_pair_ref, gate_ref, up_ref,
               after_ref, out_ref, own_rows, other_rows):
        del after_ref
        own_rows[:count] = near_ref[:, :half]
        own_rows[count:] = far_ref[:, :half]
        other_rows[:count] = near_pair_ref[:, :half]
        other_rows[count:] = far_pair_ref[:, :half]
        own = pl.multiple_of(core_ref[0] * half, half)
        other = pl.multiple_of((1 - core_ref[0]) * half, half)
        for at in range(0, units, step):
            cols = slice(at, at + step)
            w_own = jnp.concatenate(
                [gate_ref[pl.ds(own, half), cols], up_ref[pl.ds(own, half), cols]], axis=1
            )
            w_other = jnp.concatenate(
                [gate_ref[pl.ds(other, half), cols], up_ref[pl.ds(other, half), cols]], axis=1
            )
            both = jnp.dot(
                own_rows[...], w_own, preferred_element_type=jnp.float32
            ) + in_this_order(
                jnp.dot(other_rows[...], w_other, preferred_element_type=jnp.float32), count // 2
            )
            gate_out, up_out = both[:, :step], both[:, step:]
            out_ref[:, cols] = (gate_out / (1.0 + jnp.exp(-gate_out)) * up_out).astype(jnp.bfloat16)

    vmem = pl.BlockSpec(memory_space=pltpu.VMEM)
    return pl.pallas_call(
        kernel,
        in_specs=[pl.BlockSpec(memory_space=pltpu.SMEM)]
        + [vmem] * 6
        + [pl.BlockSpec(memory_space=pl.ANY)],
        scratch_shapes=[pltpu.VMEM((rows, half), jnp.bfloat16)] * 2,
        out_shape=jax.ShapeDtypeStruct((rows, units), jnp.bfloat16),
        compiler_params=pltpu.CompilerParams(vmem_limit_bytes=VMEM_BYTES),
        cost_estimate=cost(),
        name="hidden_units",
    )(core, near, near_pair, far, far_pair, gate, up, after)


def routed_outputs(core, mine, theirs, mix, down, down_pair, near, far, lanes, after):
    rows, units = mine.shape
    features = down.shape[1] // 2
    groups = units // WALSH
    count = rows // 2
    step = min(512, features)

    def kernel(core_ref, mine_ref, theirs_ref, mix_ref, down_ref, pair_ref, near_ref, far_ref,
               lanes_ref, after_ref, near_out, far_out, turned):
        del after_ref
        for g in range(groups):
            cols = slice(g * WALSH, (g + 1) * WALSH)
            both = jnp.dot(
                mine_ref[:, cols], mix_ref[:WALSH], preferred_element_type=jnp.float32
            ) + in_this_order(
                jnp.dot(theirs_ref[:, cols], mix_ref[WALSH:], preferred_element_type=jnp.float32),
                count // 2,
            )
            both = both.astype(jnp.bfloat16)
            turned[:, cols] = both[:, :WALSH]
            turned[:, units + g * WALSH : units + (g + 1) * WALSH] = both[:, WALSH:]
        tails = jnp.concatenate([near_ref[:, features:], far_ref[:, features:]], axis=0)
        route = jnp.sum(tails.astype(jnp.float32) * lanes_ref[...], axis=1, keepdims=True)
        for at in range(0, features, step):
            cols = pl.ds(pl.multiple_of(core_ref[0] * features + at, step), step)
            out = jnp.dot(
                turned[:, :units], down_ref[:, cols], preferred_element_type=jnp.float32
            ) + jnp.dot(turned[:, units:], pair_ref[:, cols], preferred_element_type=jnp.float32)
            scaled = (out * route).astype(jnp.bfloat16)
            near_out[:, at : at + step] = scaled[:count]
            far_out[:, at : at + step] = scaled[count:]

    vmem = pl.BlockSpec(memory_space=pltpu.VMEM)
    return pl.pallas_call(
        kernel,
        in_specs=[pl.BlockSpec(memory_space=pltpu.SMEM)]
        + [vmem] * 8
        + [pl.BlockSpec(memory_space=pl.ANY)],
        scratch_shapes=[pltpu.VMEM((rows, 2 * units), jnp.bfloat16)],
        out_shape=[
            jax.ShapeDtypeStruct((count, features), jnp.bfloat16),
            jax.ShapeDtypeStruct((count, features), jnp.bfloat16),
        ],
        compiler_params=pltpu.CompilerParams(vmem_limit_bytes=VMEM_BYTES),
        cost_estimate=cost(),
        name="routed_outputs",
    )(core, mine, theirs, mix, down, down_pair, near, far, lanes, after)


def spread_rows(choice, mine, back, after):
    count, features = mine.shape
    rows = choice.shape[1] // 2

    def kernel(choice_ref, mine_ref, back_ref, after_ref, keep_ref, send_ref):
        del after_ref
        both = lax.dot_general(
            choice_ref[...],
            jnp.concatenate([mine_ref[...], back_ref[...]], axis=0),
            (((0,), (0,)), ((), ())),
            preferred_element_type=jnp.float32,
        )
        keep_ref[...] = both[:rows]
        send_ref[...] = both[rows:].astype(jnp.bfloat16)

    vmem = pl.BlockSpec(memory_space=pltpu.VMEM)
    return pl.pallas_call(
        kernel,
        in_specs=[vmem, vmem, vmem, pl.BlockSpec(memory_space=pl.ANY)],
        out_shape=[
            jax.ShapeDtypeStruct((rows, features), jnp.float32),
            jax.ShapeDtypeStruct((rows, features), jnp.bfloat16),
        ],
        compiler_params=pltpu.CompilerParams(vmem_limit_bytes=VMEM_BYTES),
        cost_estimate=cost(),
        name="spread_rows",
    )(choice, mine, back, after)


def add_rows(parts, kind, after):
    def kernel(*refs):
        total = refs[0][...].astype(jnp.float32)
        for ref in refs[1 : len(parts)]:
            total = total + ref[...].astype(jnp.float32)
        refs[-1][...] = total.astype(kind)

    vmem = pl.BlockSpec(memory_space=pltpu.VMEM)
    return pl.pallas_call(
        kernel,
        in_specs=[vmem] * len(parts) + [pl.BlockSpec(memory_space=pl.ANY)],
        out_shape=jax.ShapeDtypeStruct(parts[0].shape, kind),
        compiler_params=pltpu.CompilerParams(vmem_limit_bytes=VMEM_BYTES),
        cost_estimate=cost(LIGHT),
        name="add_rows",
    )(*parts, after)


def every_expert(
    token_values, token_scales, expert_ids, route_weights, gate_weight, up_weight, down_weight
):
    experts = lax.axis_size("expert")
    core_index = lax.axis_index("tensor")
    core = core_index.astype(jnp.int32).reshape(1)
    expert = lax.axis_index("expert")
    rows, features = token_values.shape
    top = expert_ids.shape[1]
    capacity = min(rows, 5 * rows * top // (4 * experts))
    gate, up, down = gate_weight[0], up_weight[0], down_weight[0]
    first, second = (1, 2), (2, 1)
    line = experts // 4

    block = scaled_tokens(token_values, token_scales, expert_ids, route_weights, experts)
    blocks = [block]
    for index in range(1, line):
        if index % 2 == 1 and index > 1:
            blocks.append(swap(blocks[index - 1], (4, 4)))
        else:
            blocks.append(swap(block, (4 * index, 4 * index)))

    down_pair = swap(down, (0, 0), 1)

    signs = walsh_signs(WALSH) / math.sqrt(2 * WALSH)
    sign = jnp.where(core_index == 0, 1.0, -1.0)
    mix = jnp.concatenate(
        [
            jnp.concatenate([signs * sign, signs], axis=1),
            jnp.concatenate([signs, -signs * sign], axis=1),
        ],
        axis=0,
    ).astype(jnp.bfloat16)
    lane = jnp.arange(LANES, dtype=jnp.int32)[None, :]
    lanes = ((lane % experts == expert) & (lane < 2 * experts)).astype(jnp.float32)
    beyond = expert ^ jnp.where(core_index == 0, second[0], second[1])
    named = jnp.concatenate([lane == expert, lane == beyond] + [lane < 0] * 6, axis=0).astype(
        jnp.bfloat16
    )

    state = [dict() for _ in range(line)]
    last = named
    total = None

    def pick(k):
        nonlocal last
        it = state[k]
        it["mine"], away, it["choice"] = pick_rows(
            blocks[k], swap(blocks[k], first), named, capacity, last
        )
        it["mine_pair"] = swap(it["mine"], (0, 0), 1)
        it["far"] = swap(away, second)
        it["far_pair"] = swap(it["far"], (0, 0), 1)
        last = it["choice"]

    def expand_units(k):
        nonlocal last
        it = state[k]
        it["hidden"] = hidden_units(
            core, it["mine"], it["mine_pair"], it["far"], it["far_pair"], gate, up, last
        )
        it["hidden_pair"] = swap(it["hidden"], (0, 0), 1)
        last = it["hidden"]

    def contract_units(k):
        nonlocal last
        it = state[k]
        it["out"], away = routed_outputs(
            core, it["hidden"], it["hidden_pair"], mix, down, down_pair, it["mine"], it["far"],
            lanes, last,
        )
        it["back"] = swap(away, second)
        last = it["out"]

    def spread(k):
        nonlocal last
        it = state[k]
        it["keep"], away = spread_rows(it["choice"], it["out"], it["back"], last)
        it["next"] = swap(away, first)
        last = it["keep"]

    def settle(k):
        nonlocal last, total
        it = state[k]
        if k == 0:
            total = last = add_rows([it["keep"], it["next"]], jnp.float32, last)
            return
        parts = [it["keep"], it["next"]]
        if k % 2 == 1 and k > 1:
            parts.append(state[k - 1]["sent"])
        last = add_rows(parts, jnp.bfloat16, last)
        mask = 4 if k % 2 == 0 else 4 * k
        it["sent"] = swap(last, (mask, mask))

    def absorb(k):
        nonlocal last, total
        if k % 2 == 1:
            kind = jnp.bfloat16 if k == line - 1 else jnp.float32
            total = last = add_rows([total, state[k]["sent"]], kind, last)

    steps = (pick, expand_units, contract_units, spread, settle, absorb)
    due = [
        (times[min(k, 3)] + 10 * max(0, k - 3), name, k)
        for name, times in enumerate(ORDER)
        for k in range(line)
    ]
    for _, name, k in sorted(due):
        steps[name](k)
    return total


def chosen_experts(
    token_values, token_scales, expert_ids, route_weights, gate_weight, up_weight, down_weight
):
    tok_rows, top_count = expert_ids.shape
    experts = lax.axis_size("expert")
    capacity = min(tok_rows, 5 * tok_rows * top_count // (4 * experts))
    flat_ids = expert_ids.reshape(-1)
    onehot = (flat_ids[:, None] == jnp.arange(experts, dtype=jnp.int32)[None, :]).astype(jnp.int32)
    slot_index = jnp.sum(jnp.cumsum(onehot, axis=0) * onehot, axis=1) - 1
    target = flat_ids * capacity + slot_index
    owner_token = jnp.arange(tok_rows * top_count, dtype=jnp.int32) // top_count
    source = jnp.full((experts * capacity,), tok_rows, jnp.int32).at[target].set(owner_token)
    padded_values = jnp.concatenate(
        [token_values, jnp.zeros((1, token_values.shape[1]), token_values.dtype)], axis=0
    )
    padded_scales = jnp.concatenate(
        [token_scales, jnp.zeros((1, token_scales.shape[1]), token_scales.dtype)], axis=0
    )
    send_values = padded_values[source].reshape(experts, capacity, -1)
    send_scales = padded_scales[source].reshape(experts, capacity, -1)
    arrived_values, arrived_scales = (
        lax.all_to_all(send_values, "expert", split_axis=0, concat_axis=0, tiled=True),
        lax.all_to_all(send_scales, "expert", split_axis=0, concat_axis=0, tiled=True),
    )
    joined_values, joined_scales = (
        lax.all_gather(arrived_values, "tensor", axis=2, tiled=True),
        lax.all_gather(arrived_scales, "tensor", axis=2, tiled=True),
    )
    row_count = experts * capacity
    feature_count = joined_values.shape[2]
    scale_count = joined_scales.shape[2]
    dequant = (
        (
            joined_values.astype(jnp.float32).reshape(
                row_count, scale_count, feature_count // scale_count
            )
            * joined_scales.astype(jnp.float32).reshape(row_count, scale_count, 1)
        )
        .reshape(row_count, feature_count)
        .astype(jnp.bfloat16)
    )
    gate_out = jnp.dot(dequant, gate_weight[0], preferred_element_type=jnp.float32)
    up_out = jnp.dot(dequant, up_weight[0], preferred_element_type=jnp.float32)
    hidden = (jax.nn.silu(gate_out) * up_out).astype(jnp.bfloat16)
    partner = swap(hidden, (0, 0), 1)
    own_part = hidden.astype(jnp.float32)
    theirs = partner.astype(jnp.float32)
    combined = jnp.where(lax.axis_index("tensor") == 0, own_part + theirs, theirs - own_part)
    groups = hidden.shape[1] // WALSH
    norm_factor = 1.0 / math.sqrt(2 * WALSH)
    turned = (
        jnp.einsum(
            "rgj,kj->rgk",
            combined.reshape(row_count, groups, WALSH),
            walsh_signs(WALSH),
            precision=lax.Precision.HIGHEST,
        )
        * norm_factor
    )
    rotated = turned.reshape(row_count, -1).astype(jnp.bfloat16)
    partial_value = jnp.dot(rotated, down_weight[0], preferred_element_type=jnp.float32)
    summed = lax.psum_scatter(partial_value, "tensor", scatter_dimension=1, tiled=True).astype(
        jnp.bfloat16
    )
    returned = lax.all_to_all(
        summed.reshape(experts, capacity, -1), "expert", split_axis=0, concat_axis=0, tiled=True
    )
    picked = (
        returned.reshape(experts * capacity, -1)[target]
        .astype(jnp.float32)
        .reshape(tok_rows, top_count, -1)
    )
    route = route_weights.astype(jnp.float32)
    route = route / jnp.sum(route, axis=1, keepdims=True)
    return jnp.sum(picked * route[:, :, None], axis=1).astype(jnp.bfloat16)


def shards(*arrays):
    experts = lax.axis_size("expert")
    top = arrays[2].shape[1]
    dense = 2 * top >= experts and experts % 4 == 0 and experts & (experts - 1) == 0
    return (every_expert if dense else chosen_experts)(*arrays)


def solution(mesh):
    return jax.shard_map(
        shards,
        mesh=mesh,
        in_specs=(
            P(("replica", "expert"), "tensor"),
            P(("replica", "expert"), "tensor"),
            P(("replica", "expert"), None),
            P(("replica", "expert"), None),
            P("expert", None, "tensor"),
            P("expert", None, "tensor"),
            P("expert", "tensor", None),
        ),
        out_specs=P(("replica", "expert"), "tensor"),
        check_vma=False,
    )
```
